32 devices in a mesh: dp: 16 (over z, y, x), tensor: 2 (over core).
Axes of the slice: x: 2, y: 2, z: 4, core: 2. Of those that a mesh axis runs over, the one named last changes fastest.
Arguments:
- tokens: bfloat16 [4096, 8192], P('dp', 'tensor'), may hold values from -6 to 6
- norm_gain: bfloat16 [8192], P('tensor'), may hold values from 0.099609375 to 1.8984375
- kept_blocks: bfloat16 [8192, 6144], P('dp', 'tensor'), may hold values from -0.09375 to 0.09375
- block_cols: int32 [64, 48], P('dp', 'tensor'), may hold values from 0 to 39, as said below
- row_counts: int32 [64, 2], P('dp', 'tensor'), may hold values from 16 to 24, as said below
Outputs:
- projected: bfloat16 [4096, 10240], P('dp', 'tensor')
The draws below stay inside these ranges and needn't reach their ends.
Inputs may be any that keep to these rules, and one draw needn't show every extreme that they name: `block_cols`: in each row block the 24 slots of one shard name distinct column blocks of that shard, also the slots beyond row_counts. `row_counts`: in every shard some row block has 24 kept blocks.
All inputs are finite; a program needn't handle non-finite values.
Results may differ from the reference program's by a relative error of at most 0.0049.
Values may be sent and summed in bfloat16 or wider, within the bound.
A program may use at most 128 MiB of HBM per device.

```python
import jax
import jax.numpy as jnp
from jax import lax

D = 8192
GROUP = 8
HD = 128
BS = 128
TOK_DEV = 256
TOKENS = 4096
SHARDS = 2
QKV = 10240
BLK_DEV = 40
LOW = 16
CAP = 24
SLOTS = 48
RB = 64


def shared_layout(key):
    count_key, fullest_key, order_key = jax.random.split(key, 3)
    counts = jax.random.randint(count_key, (RB, SHARDS), LOW, CAP + 1)
    fullest = jax.random.randint(fullest_key, (SHARDS,), 0, RB)
    counts = jnp.where(jnp.arange(RB)[:, None] == fullest[None, :], CAP, counts)
    scores = jax.random.randint(order_key, (RB, SHARDS, BLK_DEV), 0, 1 << 20) * BLK_DEV + jnp.arange(BLK_DEV)[None, None, :]
    ranking = jnp.argsort(scores, axis=-1)
    columns = ranking[:, :, :CAP].reshape(RB, SHARDS * CAP)
    return (counts.astype(jnp.int32), columns.astype(jnp.int32))


def draw_block_cols(key, part):
    return shared_layout(jax.random.fold_in(key, 11))[1]


def draw_row_counts(key, part):
    return shared_layout(jax.random.fold_in(key, 11))[0]


def shard_levels(rng, extent, pieces, least, high):
    def one(axis_at, shards_of):
        draws = jax.random.uniform(jax.random.fold_in(jax.random.fold_in(rng, 6), axis_at), (shards_of,), jnp.float32, least / len(pieces), high / len(pieces))
        return jnp.repeat(jnp.exp(draws), extent[axis_at] // shards_of).reshape((-1,) + (1,) * (len(extent) - axis_at - 1))

    gain = one(*pieces[0])
    for cut in pieces[1:]:
        gain = gain * one(*cut)
    return gain


def normal_values(stream_key, shape, width, limit, pieces=(), kind=jnp.bfloat16):
    drawn = width * jax.random.normal(stream_key, shape, jnp.float32)
    if pieces:
        drawn = drawn * shard_levels(stream_key, shape, pieces, -0.22, 0.18)
    return jnp.clip(drawn, -limit, limit).astype(kind)


def setup_inputs(seed: int = 0) -> dict:
    key_of = jax.random.split(jax.random.key(seed), 6)
    return {
        "tokens": normal_values(key_of[0], (TOKENS, D), 1.0, 6.0, ((0, 16), (1, 2))),
        "norm_gain": jnp.clip(1.0 + 0.18 * jax.random.normal(key_of[1], (D,), jnp.float32), 0.099609375, 1.8984375).astype(jnp.bfloat16),
        "kept_blocks": normal_values(key_of[2], (D, SLOTS * BS), (D // 2) ** -0.5, 0.09375, ((0, 16), (1, 2))),
        "block_cols": draw_block_cols(jax.random.fold_in(key_of[5], 71), 0),
        "row_counts": draw_row_counts(jax.random.fold_in(key_of[5], 71), 0),
    }


rope_theta = 500000.0

def rotate(mixed, positions):
    row_count = mixed.shape[0]
    head_view = mixed.reshape(row_count, -1, GROUP + 2, HD)
    half_size = HD // 2
    inverse_freq = rope_theta ** (-(jnp.arange(half_size).astype(jnp.float32) * 2.0 / HD))
    angles = positions[:, None] * inverse_freq[None, :]
    cosine = jnp.cos(angles)[:, None, None, :]
    sine_part = jnp.sin(angles)[:, None, None, :]
    first_half = head_view[..., :half_size]
    second = head_view[..., half_size:]
    turned = jnp.concatenate([first_half * cosine - second * sine_part, second * cosine + first_half * sine_part], axis=-1)
    rotated_heads = (jnp.arange(GROUP + 2) < GROUP + 1)[None, None, :, None]
    return jnp.where(rotated_heads, turned, head_view).reshape(row_count, -1)

def reference(tokens, norm_gain, kept_blocks, block_cols, row_counts):
    shards = SLOTS // CAP
    floats = tokens.astype(jnp.float32)
    mean_square = lax.optimization_barrier(jnp.mean(floats * floats, axis=-1, keepdims=True))
    normed = (floats * lax.rsqrt(mean_square + 1e-05) * norm_gain.astype(jnp.float32)).astype(jnp.bfloat16)
    blocks = kept_blocks.reshape(RB, BS, shards, CAP, BS)
    columns = block_cols.reshape(RB, shards, CAP)
    filled = jnp.arange(CAP)[None, None, :] < row_counts[:, :, None]
    placing = ((columns[:, :, :, None] == jnp.arange(BLK_DEV)[None, None, None, :]) & filled[..., None]).astype(jnp.float32)
    positions = (jnp.arange(TOKENS) % TOK_DEV).astype(jnp.float32)

    def one_shard(shard_index):
        shard_blocks = lax.dynamic_index_in_dim(blocks, shard_index, 2, keepdims=False).astype(jnp.float32)
        shard_place = lax.dynamic_index_in_dim(placing, shard_index, 1, keepdims=False)
        dense_rows = jnp.einsum('rksj,rsc->rkcj', shard_blocks, shard_place).astype(jnp.bfloat16).reshape(D, BLK_DEV * BS)
        mixed = jnp.dot(normed, dense_rows, preferred_element_type=jnp.float32)
        return rotate(mixed, positions).astype(jnp.bfloat16)
    results = lax.map(one_shard, jnp.arange(shards))
    return jnp.transpose(results, (1, 0, 2)).reshape(TOKENS, QKV)
```

```python
import functools

import jax
import jax.numpy as jnp
from jax import lax
from jax.experimental import pallas as pl
from jax.experimental.pallas import tpu as pltpu
from jax.sharding import PartitionSpec as P

KVH = 8
GROUP = 8
HD = 128
BS = 128


rope_theta = 500000.0


def rotate(mixed, positions):
    row_count = mixed.shape[0]
    head_view = mixed.reshape(row_count, -1, HD)
    heads = head_view.shape[1]
    half_size = HD // 2
    inverse_freq = rope_theta ** (-(jnp.arange(half_size).astype(jnp.float32) * 2.0 / HD))
    angles = positions[:, None] * inverse_freq[None, :]
    cosine = jnp.cos(angles)
    sine_part = jnp.sin(angles)
    cos_full = jnp.concatenate([cosine, cosine], axis=-1)[:, None, :]
    sin_full = jnp.concatenate([-sine_part, sine_part], axis=-1)[:, None, :]
    swapped = jnp.roll(head_view, half_size, axis=-1)
    turned = head_view * cos_full + swapped * sin_full
    rotated_heads = (jnp.arange(heads) % (GROUP + 2) < GROUP + 1)[None, :, None]
    return jnp.where(rotated_heads, turned, head_view).reshape(row_count, -1)


def place_body(where_ref, blocks_ref, *rest, slots, column_blocks):
    out_ref = rest[-1]
    row = pl.program_id(0)
    for column in range(column_blocks):
        slot = where_ref[1 + row * column_blocks + column]
        start = pl.multiple_of(jnp.minimum(slot, slots - 1) * BS, BS)
        block = blocks_ref[:, pl.ds(start, BS)]
        out_ref[:, column * BS : (column + 1) * BS] = jnp.where(
            slot < slots, block, jnp.zeros_like(block)
        )


def place(where, blocks, dense, total_rows, column_blocks):
    rows, width = blocks.shape
    slots = width // BS
    in_specs = [pl.BlockSpec((BS, width), lambda r, where: (r, 0))]
    operands = [where, blocks]
    aliases = {}
    if dense is not None:
        in_specs.append(pl.BlockSpec(memory_space=pl.ANY))
        operands.append(dense)
        aliases = {2: 0}
    return pl.pallas_call(
        functools.partial(place_body, slots=slots, column_blocks=column_blocks),
        grid_spec=pltpu.PrefetchScalarGridSpec(
            num_scalar_prefetch=1,
            grid=(rows // BS,),
            in_specs=in_specs,
            out_specs=pl.BlockSpec((BS, column_blocks * BS), lambda r, where: (where[0] + r, 0)),
        ),
        out_shape=jax.ShapeDtypeStruct((total_rows, column_blocks * BS), jnp.bfloat16),
        input_output_aliases=aliases,
        compiler_params=pltpu.CompilerParams(vmem_limit_bytes=16 * 1024 * 1024),
        cost_estimate=pl.CostEstimate(
            flops=0, bytes_accessed=rows * (width + column_blocks * BS) * 2, transcendentals=0
        ),
    )(*operands)


def per_device(tokens, norm_gain, kept_blocks, block_cols, row_counts):
    tensor_count = lax.axis_size("tensor")
    devices = lax.axis_size("dp")
    me = lax.axis_index("dp")
    column_blocks = KVH // tensor_count * (GROUP + 2) * HD // BS
    rows_here, slots = block_cols.shape
    shard_rows = rows_here * BS
    seq = tokens.shape[0]
    bits = devices.bit_length() - 1
    y_mask, z_mask = 2, 4
    across = [1 << b for b in range(bits - 1, -1, -1) if (1 << b) not in (y_mask, z_mask)]
    group = devices // 4

    def swap(value, mask):
        return lax.ppermute(value, "dp", [(i, i ^ mask) for i in range(devices)])

    def position(index):
        return index // 8 * 2 + index % 2

    slot_of = jnp.where(
        (block_cols[:, None, :] == jnp.arange(column_blocks)[None, :, None])
        & (jnp.arange(slots)[None, None, :] < row_counts[:, :, None]),
        jnp.arange(slots)[None, None, :] - slots,
        0,
    )
    slot_of = (jnp.sum(slot_of, axis=-1) + slots).astype(jnp.int32)
    slot_all = lax.all_gather(slot_of, "dp", axis=0)

    pieces = {0: kept_blocks}
    for mask in across:
        for known in list(pieces):
            if known == 0:
                pieces[mask] = swap(kept_blocks, mask)
        for known in list(pieces):
            if known not in (0, mask) and known ^ mask not in pieces:
                pieces[known ^ mask] = swap(pieces[known], mask)

    gathered, gain_all = (
        lax.all_gather(tokens, "tensor", axis=1, tiled=True),
        lax.all_gather(norm_gain, "tensor", axis=0, tiled=True),
    )
    floats = gathered.astype(jnp.float32)
    mean_square = jnp.mean(floats * floats, axis=-1, keepdims=True)
    normed = (floats * lax.rsqrt(mean_square + 1e-05) * gain_all.astype(jnp.float32)).astype(
        jnp.bfloat16
    )
    by_owner = normed.reshape(seq, devices // 8, 4, 2, shard_rows)

    def features_of(index):
        part = lax.dynamic_slice_in_dim(by_owner, index % 8 // 2, 1, 2)
        return part.reshape(seq, group * shard_rows)

    d_mask = y_mask | z_mask
    x_far = swap(features_of(me ^ d_mask), d_mask)
    x_y = swap(features_of(me ^ y_mask), y_mask)
    x_z = swap(features_of(me ^ z_mask), z_mask)
    x_own = features_of(me)

    dense = None
    for mask, blocks in pieces.items():
        peer = me ^ mask
        where = jnp.concatenate(
            [
                (position(peer) * rows_here).reshape(1).astype(jnp.int32),
                lax.dynamic_index_in_dim(slot_all, peer, 0, keepdims=False).reshape(-1),
            ]
        )
        dense = place(where, blocks, dense, group * shard_rows, column_blocks)

    def product(left):
        return jnp.dot(left, dense, preferred_element_type=jnp.float32)

    half = column_blocks * BS // 2
    far = product(x_far).astype(jnp.bfloat16)
    via_y = swap(far[:, :half], y_mask)
    via_z = swap(far[:, half:], z_mask)
    part_y = product(x_y)
    y_first = swap(part_y[:, :half].astype(jnp.bfloat16), y_mask)
    part_z = product(x_z)
    z_second = swap(part_z[:, half:].astype(jnp.bfloat16), z_mask)
    y_second = swap(
        (part_y[:, half:] + via_z.astype(jnp.float32)).astype(jnp.bfloat16), y_mask
    )
    z_first = swap(
        (part_z[:, :half] + via_y.astype(jnp.float32)).astype(jnp.bfloat16), z_mask
    )
    own = product(x_own)
    first = own[:, :half] + y_first.astype(jnp.float32) + z_first.astype(jnp.float32)
    second = own[:, half:] + y_second.astype(jnp.float32) + z_second.astype(jnp.float32)
    positions = jnp.arange(seq).astype(jnp.float32)
    return rotate(jnp.concatenate([first, second], axis=1), positions).astype(jnp.bfloat16)


def solution(mesh):
    in_specs = (
        P("dp", "tensor"),
        P("tensor"),
        P("dp", "tensor"),
        P("dp", "tensor"),
        P("dp", "tensor"),
    )
    out_specs = P("dp", "tensor")
    return jax.shard_map(
        per_device, mesh=mesh, in_specs=in_specs, out_specs=out_specs, check_vma=False
    )
```

```python
import functools

import jax
import jax.numpy as jnp
from jax import lax
from jax.experimental import pallas as pl
from jax.experimental.pallas import tpu as pltpu
from jax.sharding import PartitionSpec as P

KVH = 8
GROUP = 8
HD = 128
BS = 128


rope_theta = 500000.0


def place_body(where_ref, blocks_ref, *rest, slots, column_blocks):
    out_ref = rest[-1]
    row = pl.program_id(0)
    for column in range(column_blocks):
        slot = where_ref[1 + row * column_blocks + column]
        start = pl.multiple_of(jnp.minimum(slot, slots - 1) * BS, BS)
        block = blocks_ref[:, pl.ds(start, BS)]
        out_ref[:, column * BS : (column + 1) * BS] = jnp.where(
            slot < slots, block, jnp.zeros_like(block)
        )


def place(where, blocks, dense, total_rows, column_blocks):
    rows, width = blocks.shape
    slots = width // BS
    in_specs = [pl.BlockSpec((BS, width), lambda r, where: (r, 0))]
    operands = [where, blocks]
    aliases = {}
    if dense is not None:
        in_specs.append(pl.BlockSpec(memory_space=pl.ANY))
        operands.append(dense)
        aliases = {2: 0}
    return pl.pallas_call(
        functools.partial(place_body, slots=slots, column_blocks=column_blocks),
        grid_spec=pltpu.PrefetchScalarGridSpec(
            num_scalar_prefetch=1,
            grid=(rows // BS,),
            in_specs=in_specs,
            out_specs=pl.BlockSpec((BS, column_blocks * BS), lambda r, where: (where[0] + r, 0)),
        ),
        out_shape=jax.ShapeDtypeStruct((total_rows, column_blocks * BS), jnp.bfloat16),
        input_output_aliases=aliases,
        compiler_params=pltpu.CompilerParams(vmem_limit_bytes=56 * 1024 * 1024),
        cost_estimate=pl.CostEstimate(
            flops=0, bytes_accessed=rows * (width + column_blocks * BS) * 2, transcendentals=0
        ),
    )(*operands)


def finish_body(own, a_first, a_second, z_first, z_second, cosine, sine, out_ref, *, steps, heads):
    step = pl.program_id(0)
    cos_here = cosine[...]
    sin_here = sine[...]

    def write(from_a, from_z):
        for head in range(heads):
            lanes = slice(head * HD, (head + 1) * HD)
            mixed = (
                own[:, lanes]
                + from_a[:, lanes].astype(jnp.float32)
                + from_z[:, lanes].astype(jnp.float32)
            )
            turned = mixed * cos_here + pltpu.roll(mixed, HD // 2, 1) * sin_here
            rotated = (step * heads + head) % (GROUP + 2) < GROUP + 1
            out_ref[:, lanes] = jnp.where(rotated, turned, mixed).astype(jnp.bfloat16)

    @pl.when(step < steps // 2)
    def _():
        write(a_first, z_first)

    @pl.when(step >= steps // 2)
    def _():
        write(a_second, z_second)


def finish(own, a_first, a_second, z_first, z_second):
    rows, width = own.shape
    heads = (GROUP + 2) // 2
    block = heads * HD
    steps = width // block
    half_steps = steps // 2
    half_size = HD // 2
    inverse_freq = rope_theta ** (-(jnp.arange(half_size).astype(jnp.float32) * 2.0 / HD))
    angles = jnp.arange(rows).astype(jnp.float32)[:, None] * inverse_freq[None, :]
    cosine = jnp.cos(angles)
    sine = jnp.sin(angles)
    cos_full = jnp.concatenate([cosine, cosine], axis=-1)
    sin_full = jnp.concatenate([-sine, sine], axis=-1)
    low = pl.BlockSpec((rows, block), lambda j: (0, jnp.minimum(j, half_steps - 1)))
    high = pl.BlockSpec((rows, block), lambda j: (0, jnp.maximum(j - half_steps, 0)))
    table = pl.BlockSpec((rows, HD), lambda j: (0, 0))
    return pl.pallas_call(
        functools.partial(finish_body, steps=steps, heads=heads),
        grid=(steps,),
        in_specs=[pl.BlockSpec((rows, block), lambda j: (0, j)), low, high, low, high, table, table],
        out_specs=pl.BlockSpec((rows, block), lambda j: (0, j)),
        out_shape=jax.ShapeDtypeStruct((rows, width), jnp.bfloat16),
        compiler_params=pltpu.CompilerParams(vmem_limit_bytes=48 * 1024 * 1024),
        cost_estimate=pl.CostEstimate(
            flops=rows * width * 6, bytes_accessed=rows * width * 10, transcendentals=0
        ),
    )(own, a_first, a_second, z_first, z_second, cos_full, sin_full)


def per_device(tokens, norm_gain, kept_blocks, block_cols, row_counts):
    tensor_count = lax.axis_size("tensor")
    devices = lax.axis_size("dp")
    me = lax.axis_index("dp")
    column_blocks = KVH // tensor_count * (GROUP + 2) * HD // BS
    rows_here, slots = block_cols.shape
    shard_rows = rows_here * BS
    group = devices // 4
    odd = lax.axis_index("tensor") % 2
    z_bit = (4, 4)
    sum_bit = (2, 1)
    weight_bit = (1, 2)
    far_bits = (6, 5)
    across = [(1 << b, 1 << b) for b in range(devices.bit_length() - 2, 2, -1)]

    def swap(value, masks):
        pairs = [
            (i * tensor_count + t, (i ^ masks[t % 2]) * tensor_count + t)
            for i in range(devices)
            for t in range(tensor_count)
        ]
        return lax.ppermute(value, ("dp", "tensor"), pairs)

    def mine(masks):
        return jnp.where(odd == 1, masks[1], masks[0])

    def position(index):
        return index // 8 * 2 + jnp.where(index & mine(weight_bit) > 0, 1, 0)

    offsets = [(0, 0)]
    for masks in across:
        offsets += [(e ^ masks[0], o ^ masks[1]) for e, o in offsets]
    offsets += [(e ^ weight_bit[0], o ^ weight_bit[1]) for e, o in offsets]

    slot_of = jnp.where(
        (block_cols[:, None, :] == jnp.arange(column_blocks)[None, :, None])
        & (jnp.arange(slots)[None, None, :] < row_counts[:, :, None]),
        jnp.arange(slots)[None, None, :] - slots,
        0,
    )
    slot_of = (jnp.sum(slot_of, axis=-1) + slots).astype(jnp.int32)
    slots_from = [slot_of] + [swap(slot_of, masks) for masks in offsets[1:]]
    tied = lax.optimization_barrier([kept_blocks] + slots_from)
    kept_blocks, slots_from = tied[0], tied[1:]

    order = []
    for row in range(rows_here):
        chunk = kept_blocks[row * BS : (row + 1) * BS]
        held = {(0, 0): chunk}
        for masks in across:
            for known in list(held):
                held[(known[0] ^ masks[0], known[1] ^ masks[1])] = swap(held[known], masks)
        for known in list(held):
            held[(known[0] ^ weight_bit[0], known[1] ^ weight_bit[1])] = swap(
                held[known], weight_bit
            )
        order += [(row, masks, held[masks]) for masks in offsets]

    gathered, gain_all = (
        lax.all_gather(tokens, "tensor", axis=1, tiled=True),
        lax.all_gather(norm_gain, "tensor", axis=0, tiled=True),
    )
    floats = gathered.astype(jnp.float32)
    mean_square = jnp.mean(floats * floats, axis=-1, keepdims=True)
    normed = (floats * lax.rsqrt(mean_square + 1e-05) * gain_all.astype(jnp.float32)).astype(
        jnp.bfloat16
    )

    def features_of(index):
        fixed = index & mine(far_bits)
        parts = []
        for place_at in range(group):
            owner = fixed + place_at // 2 * 8 + place_at % 2 * mine(weight_bit)
            parts.append(lax.dynamic_slice_in_dim(normed, owner * shard_rows, shard_rows, 1))
        return jnp.concatenate(parts, axis=1)

    x_far = swap(features_of(me ^ mine(far_bits)), far_bits)
    x_z = swap(features_of(me ^ 4), z_bit)
    x_a = swap(features_of(me ^ mine(sum_bit)), sum_bit)
    x_own = features_of(me)

    dense = None
    slot_table = dict(zip(offsets, slots_from))
    for row, masks, blocks in order:
        peer = me ^ mine(masks)
        where = jnp.concatenate(
            [
                (position(peer) * rows_here + row).reshape(1).astype(jnp.int32),
                slot_table[masks][row],
            ]
        )
        dense = place(where, blocks, dense, group * shard_rows, column_blocks)

    def product(left):
        return jnp.dot(left, dense, preferred_element_type=jnp.float32)

    half = column_blocks * BS // 2
    far = product(x_far).astype(jnp.bfloat16)
    far_first = swap(far[:, :half], sum_bit)
    far_second = swap(far[:, half:], sum_bit)
    part_z = product(x_z)
    part_a = product(x_a).astype(jnp.bfloat16)
    a_first = swap(part_a[:, :half], sum_bit)
    a_second = swap(part_a[:, half:], sum_bit)
    z_first = swap(
        (part_z[:, :half] + far_first.astype(jnp.float32)).astype(jnp.bfloat16), z_bit
    )
    z_second = swap(
        (part_z[:, half:] + far_second.astype(jnp.float32)).astype(jnp.bfloat16), z_bit
    )
    return finish(product(x_own), a_first, a_second, z_first, z_second)


def solution(mesh):
    in_specs = (
        P("dp", "tensor"),
        P("tensor"),
        P("dp", "tensor"),
        P("dp", "tensor"),
        P("dp", "tensor"),
    )
    out_specs = P("dp", "tensor")
    return jax.shard_map(
        per_device, mesh=mesh, in_specs=in_specs, out_specs=out_specs, check_vma=False
    )
```

```python
import functools

import jax
import jax.numpy as jnp
from jax import lax
from jax.experimental import pallas as pl
from jax.experimental.pallas import tpu as pltpu
from jax.sharding import PartitionSpec as P

KVH = 8
GROUP = 8
HD = 128
BS = 128


rope_theta = 500000.0


def place_body(where_ref, blocks_ref, *rest, slots, column_blocks):
    out_ref = rest[-1]
    row = pl.program_id(0)
    for column in range(column_blocks):
        slot = where_ref[1 + row * column_blocks + column]
        start = pl.multiple_of(jnp.minimum(slot, slots - 1) * BS, BS)
        block = blocks_ref[:, pl.ds(start, BS)]
        out_ref[:, column * BS : (column + 1) * BS] = jnp.where(
            slot < slots, block, jnp.zeros_like(block)
        )


def place(where, blocks, dense, total_rows, column_blocks):
    rows, width = blocks.shape
    slots = width // BS
    in_specs = [pl.BlockSpec((BS, width), lambda r, where: (r, 0))]
    operands = [where, blocks]
    aliases = {}
    if dense is not None:
        in_specs.append(pl.BlockSpec(memory_space=pl.ANY))
        operands.append(dense)
        aliases = {2: 0}
    return pl.pallas_call(
        functools.partial(place_body, slots=slots, column_blocks=column_blocks),
        grid_spec=pltpu.PrefetchScalarGridSpec(
            num_scalar_prefetch=1,
            grid=(rows // BS,),
            in_specs=in_specs,
            out_specs=pl.BlockSpec((BS, column_blocks * BS), lambda r, where: (where[0] + r, 0)),
        ),
        out_shape=jax.ShapeDtypeStruct((total_rows, column_blocks * BS), jnp.bfloat16),
        input_output_aliases=aliases,
        compiler_params=pltpu.CompilerParams(vmem_limit_bytes=56 * 1024 * 1024),
        cost_estimate=pl.CostEstimate(
            flops=0, bytes_accessed=rows * (width + column_blocks * BS) * 2, transcendentals=0
        ),
    )(*operands)


def finish_body(own, a_first, a_second, z_first, z_second, cosine, sine, out_ref, *, steps, heads):
    step = pl.program_id(0)
    cos_here = cosine[...]
    sin_here = sine[...]

    def write(from_a, from_z):
        for head in range(heads):
            lanes = slice(head * HD, (head + 1) * HD)
            mixed = (
                own[:, lanes]
                + from_a[:, lanes].astype(jnp.float32)
                + from_z[:, lanes].astype(jnp.float32)
            )
            turned = mixed * cos_here + pltpu.roll(mixed, HD // 2, 1) * sin_here
            rotated = (step * heads + head) % (GROUP + 2) < GROUP + 1
            out_ref[:, lanes] = jnp.where(rotated, turned, mixed).astype(jnp.bfloat16)

    @pl.when(step < steps // 2)
    def _():
        write(a_first, z_first)

    @pl.when(step >= steps // 2)
    def _():
        write(a_second, z_second)


def finish(own, a_first, a_second, z_first, z_second):
    rows, width = own.shape
    heads = (GROUP + 2) // 2
    block = heads * HD
    steps = width // block
    half_steps = steps // 2
    half_size = HD // 2
    inverse_freq = rope_theta ** (-(jnp.arange(half_size).astype(jnp.float32) * 2.0 / HD))
    angles = jnp.arange(rows).astype(jnp.float32)[:, None] * inverse_freq[None, :]
    cosine = jnp.cos(angles)
    sine = jnp.sin(angles)
    cos_full = jnp.concatenate([cosine, cosine], axis=-1)
    sin_full = jnp.concatenate([-sine, sine], axis=-1)
    low = pl.BlockSpec((rows, block), lambda j: (0, jnp.minimum(j, half_steps - 1)))
    high = pl.BlockSpec((rows, block), lambda j: (0, jnp.maximum(j - half_steps, 0)))
    table = pl.BlockSpec((rows, HD), lambda j: (0, 0))
    return pl.pallas_call(
        functools.partial(finish_body, steps=steps, heads=heads),
        grid=(steps,),
        in_specs=[pl.BlockSpec((rows, block), lambda j: (0, j)), low, high, low, high, table, table],
        out_specs=pl.BlockSpec((rows, block), lambda j: (0, j)),
        out_shape=jax.ShapeDtypeStruct((rows, width), jnp.bfloat16),
        compiler_params=pltpu.CompilerParams(vmem_limit_bytes=48 * 1024 * 1024),
        cost_estimate=pl.CostEstimate(
            flops=rows * width * 6, bytes_accessed=rows * width * 10, transcendentals=0
        ),
    )(own, a_first, a_second, z_first, z_second, cos_full, sin_full)


def per_device(tokens, norm_gain, kept_blocks, block_cols, row_counts):
    tensor_count = lax.axis_size("tensor")
    devices = lax.axis_size("dp")
    me = lax.axis_index("dp")
    column_blocks = KVH // tensor_count * (GROUP + 2) * HD // BS
    rows_here, slots = block_cols.shape
    shard_rows = rows_here * BS
    group = devices // 4
    odd = lax.axis_index("tensor") % 2
    z_bit = (4, 4)
    sum_bit = (2, 1)
    weight_bit = (1, 2)
    far_bits = (6, 5)
    across = [(1 << b, 1 << b) for b in range(devices.bit_length() - 2, 2, -1)]

    def swap(value, masks):
        pairs = [
            (i * tensor_count + t, (i ^ masks[t % 2]) * tensor_count + t)
            for i in range(devices)
            for t in range(tensor_count)
        ]
        return lax.ppermute(value, ("dp", "tensor"), pairs)

    def mine(masks):
        return jnp.where(odd == 1, masks[1], masks[0])

    def position(index):
        return index // 8 * 2 + jnp.where(index & mine(weight_bit) > 0, 1, 0)

    offsets = [(0, 0)]
    for masks in across:
        offsets += [(e ^ masks[0], o ^ masks[1]) for e, o in offsets]
    offsets += [(e ^ weight_bit[0], o ^ weight_bit[1]) for e, o in offsets]

    slot_of = jnp.where(
        (block_cols[:, None, :] == jnp.arange(column_blocks)[None, :, None])
        & (jnp.arange(slots)[None, None, :] < row_counts[:, :, None]),
        jnp.arange(slots)[None, None, :] - slots,
        0,
    )
    slot_of = (jnp.sum(slot_of, axis=-1) + slots).astype(jnp.int32)
    slots_from = [slot_of] + [swap(slot_of, masks) for masks in offsets[1:]]
    tied = lax.optimization_barrier([kept_blocks] + slots_from)
    kept_blocks, slots_from = tied[0], tied[1:]

    gathered, gain_all = (
        lax.all_gather(tokens, "tensor", axis=1, tiled=True),
        lax.all_gather(norm_gain, "tensor", axis=0, tiled=True),
    )
    floats = gathered.astype(jnp.float32)
    mean_square = jnp.mean(floats * floats, axis=-1, keepdims=True)
    normed = (floats * lax.rsqrt(mean_square + 1e-05) * gain_all.astype(jnp.float32)).astype(
        jnp.bfloat16
    )

    def features_of(index):
        fixed = index & mine(far_bits)
        parts = []
        for place_at in range(group):
            owner = fixed + place_at // 2 * 8 + place_at % 2 * mine(weight_bit)
            parts.append(lax.dynamic_slice_in_dim(normed, owner * shard_rows, shard_rows, 1))
        return jnp.concatenate(parts, axis=1)

    x_far = swap(features_of(me ^ mine(far_bits)), far_bits)
    x_z = swap(features_of(me ^ 4), z_bit)
    x_a = swap(features_of(me ^ mine(sum_bit)), sum_bit)
    x_own = features_of(me)

    slot_table = dict(zip(offsets, slots_from))

    def put(masks, row, blocks, dense):
        where = jnp.concatenate(
            [
                (position(me ^ mine(masks)) * rows_here + row).reshape(1).astype(jnp.int32),
                slot_table[masks][row : row + blocks.shape[0] // BS].reshape(-1),
            ]
        )
        return place(where, blocks, dense, group * shard_rows, column_blocks)

    def plus(masks, more):
        return (masks[0] ^ more[0], masks[1] ^ more[1])

    near = swap(kept_blocks, weight_bit)
    chunks = []
    for row in range(rows_here):
        held = {(0, 0): kept_blocks[row * BS : (row + 1) * BS]}
        for masks in across:
            for known in list(held):
                held[plus(known, masks)] = swap(held[known], masks)
        del held[(0, 0)]
        chunks.append(held)
    dense = put((0, 0), 0, kept_blocks, None)
    late = []
    tie = [x_far, x_z, x_a]
    for row, held in enumerate(chunks):
        names = list(held)
        tied = lax.optimization_barrier([held[name] for name in names] + tie + [dense])
        if row == 0:
            x_far, x_z, x_a = tied[-4:-1]
        dense = tied[-1]
        tie = []
        if row == 1 or rows_here == 1:
            dense = put(weight_bit, 0, near, dense)
        for masks, blocks, row_of in late:
            dense = put(masks, row_of, blocks, dense)
        late = []
        for name, blocks in zip(names, tied):
            late.append((plus(name, weight_bit), swap(blocks, weight_bit), row))
            dense = put(name, row, blocks, dense)
    for masks, blocks, row_of in late:
        dense = put(masks, row_of, blocks, dense)

    def product(left):
        return jnp.dot(left, dense, preferred_element_type=jnp.float32)

    half = column_blocks * BS // 2
    far = product(x_far).astype(jnp.bfloat16)
    far, x_z, x_a = lax.optimization_barrier((far, x_z, x_a))
    far_first = swap(far[:, :half], sum_bit)
    far_second = swap(far[:, half:], sum_bit)
    part_z = product(x_z)
    part_z, x_a, x_own = lax.optimization_barrier((part_z, x_a, x_own))
    part_a = product(x_a).astype(jnp.bfloat16)
    a_first = swap(part_a[:, :half], sum_bit)
    a_second = swap(part_a[:, half:], sum_bit)
    sum_first = (part_z[:, :half] + far_first.astype(jnp.float32)).astype(jnp.bfloat16)
    sum_first, far_second = lax.optimization_barrier((sum_first, far_second))
    z_first = swap(sum_first, z_bit)
    sum_second = (part_z[:, half:] + far_second.astype(jnp.float32)).astype(jnp.bfloat16)
    z_second = swap(sum_second, z_bit)
    return finish(product(x_own), a_first, a_second, z_first, z_second)


def solution(mesh):
    in_specs = (
        P("dp", "tensor"),
        P("tensor"),
        P("dp", "tensor"),
        P("dp", "tensor"),
        P("dp", "tensor"),
    )
    out_specs = P("dp", "tensor")
    return jax.shard_map(
        per_device, mesh=mesh, in_specs=in_specs, out_specs=out_specs, check_vma=False
    )
```

```python
import functools

import jax
import jax.numpy as jnp
from jax import lax
from jax.experimental import pallas as pl
from jax.experimental.pallas import tpu as pltpu
from jax.sharding import PartitionSpec as P

KVH = 8
GROUP = 8
HD = 128
BS = 128


rope_theta = 500000.0


def place_body(where_ref, blocks_ref, *rest, slots, column_blocks):
    out_ref = rest[-1]
    row = pl.program_id(0)
    for column in range(column_blocks):
        slot = where_ref[1 + row * column_blocks + column]
        start = pl.multiple_of(jnp.minimum(slot, slots - 1) * BS, BS)
        block = blocks_ref[:, pl.ds(start, BS)]
        out_ref[:, column * BS : (column + 1) * BS] = jnp.where(
            slot < slots, block, jnp.zeros_like(block)
        )


def place(where, blocks, dense, total_rows, column_blocks):
    rows, width = blocks.shape
    slots = width // BS
    in_specs = [pl.BlockSpec((BS, width), lambda r, where: (r, 0))]
    operands = [where, blocks]
    aliases = {}
    if dense is not None:
        in_specs.append(pl.BlockSpec(memory_space=pl.ANY))
        operands.append(dense)
        aliases = {2: 0}
    return pl.pallas_call(
        functools.partial(place_body, slots=slots, column_blocks=column_blocks),
        grid_spec=pltpu.PrefetchScalarGridSpec(
            num_scalar_prefetch=1,
            grid=(rows // BS,),
            in_specs=in_specs,
            out_specs=pl.BlockSpec((BS, column_blocks * BS), lambda r, where: (where[0] + r, 0)),
        ),
        out_shape=jax.ShapeDtypeStruct((total_rows, column_blocks * BS), jnp.bfloat16),
        input_output_aliases=aliases,
        compiler_params=pltpu.CompilerParams(vmem_limit_bytes=56 * 1024 * 1024),
        cost_estimate=pl.CostEstimate(
            flops=0, bytes_accessed=rows * (width + column_blocks * BS) * 2, transcendentals=0
        ),
    )(*operands)


def finish_body(own, a_first, a_second, z_first, z_second, cosine, sine, out_ref, *, steps, heads):
    step = pl.program_id(0)
    cos_here = cosine[...]
    sin_here = sine[...]

    def write(from_a, from_z):
        for head in range(heads):
            lanes = slice(head * HD, (head + 1) * HD)
            mixed = (
                own[:, lanes]
                + from_a[:, lanes].astype(jnp.float32)
                + from_z[:, lanes].astype(jnp.float32)
            )
            turned = mixed * cos_here + pltpu.roll(mixed, HD // 2, 1) * sin_here
            rotated = (step * heads + head) % (GROUP + 2) < GROUP + 1
            out_ref[:, lanes] = jnp.where(rotated, turned, mixed).astype(jnp.bfloat16)

    @pl.when(step < steps // 2)
    def _():
        write(a_first, z_first)

    @pl.when(step >= steps // 2)
    def _():
        write(a_second, z_second)


def finish(own, a_first, a_second, z_first, z_second):
    rows, width = own.shape
    heads = (GROUP + 2) // 2
    block = heads * HD
    steps = width // block
    half_steps = steps // 2
    half_size = HD // 2
    inverse_freq = rope_theta ** (-(jnp.arange(half_size).astype(jnp.float32) * 2.0 / HD))
    angles = jnp.arange(rows).astype(jnp.float32)[:, None] * inverse_freq[None, :]
    cosine = jnp.cos(angles)
    sine = jnp.sin(angles)
    cos_full = jnp.concatenate([cosine, cosine], axis=-1)
    sin_full = jnp.concatenate([-sine, sine], axis=-1)
    low = pl.BlockSpec((rows, block), lambda j: (0, jnp.minimum(j, half_steps - 1)))
    high = pl.BlockSpec((rows, block), lambda j: (0, jnp.maximum(j - half_steps, 0)))
    table = pl.BlockSpec((rows, HD), lambda j: (0, 0))
    return pl.pallas_call(
        functools.partial(finish_body, steps=steps, heads=heads),
        grid=(steps,),
        in_specs=[pl.BlockSpec((rows, block), lambda j: (0, j)), low, high, low, high, table, table],
        out_specs=pl.BlockSpec((rows, block), lambda j: (0, j)),
        out_shape=jax.ShapeDtypeStruct((rows, width), jnp.bfloat16),
        compiler_params=pltpu.CompilerParams(vmem_limit_bytes=48 * 1024 * 1024),
        cost_estimate=pl.CostEstimate(
            flops=rows * width * 6, bytes_accessed=rows * width * 10, transcendentals=0
        ),
    )(own, a_first, a_second, z_first, z_second, cos_full, sin_full)


def per_device(tokens, norm_gain, kept_blocks, block_cols, row_counts):
    tensor_count = lax.axis_size("tensor")
    devices = lax.axis_size("dp")
    me = lax.axis_index("dp")
    column_blocks = KVH // tensor_count * (GROUP + 2) * HD // BS
    rows_here, slots = block_cols.shape
    shard_rows = rows_here * BS
    group = devices // 4
    odd = lax.axis_index("tensor") % 2
    z_bit = (4, 4)
    sum_bit = (2, 1)
    weight_bit = (1, 2)
    far_bits = (6, 5)
    across = [(1 << b, 1 << b) for b in range(devices.bit_length() - 2, 2, -1)]

    def swap(value, masks):
        pairs = [
            (i * tensor_count + t, (i ^ masks[t % 2]) * tensor_count + t)
            for i in range(devices)
            for t in range(tensor_count)
        ]
        return lax.ppermute(value, ("dp", "tensor"), pairs)

    def mine(masks):
        return jnp.where(odd == 1, masks[1], masks[0])

    def position(index):
        return index // 8 * 2 + jnp.where(index & mine(weight_bit) > 0, 1, 0)

    offsets = [(0, 0)]
    for masks in across:
        offsets += [(e ^ masks[0], o ^ masks[1]) for e, o in offsets]
    offsets += [(e ^ weight_bit[0], o ^ weight_bit[1]) for e, o in offsets]

    slot_of = jnp.where(
        (block_cols[:, None, :] == jnp.arange(column_blocks)[None, :, None])
        & (jnp.arange(slots)[None, None, :] < row_counts[:, :, None]),
        jnp.arange(slots)[None, None, :] - slots,
        0,
    )
    slot_of = (jnp.sum(slot_of, axis=-1) + slots).astype(jnp.int32)
    slots_from = [slot_of] + [swap(slot_of, masks) for masks in offsets[1:]]
    tied = lax.optimization_barrier([kept_blocks] + slots_from)
    kept_blocks, slots_from = tied[0], tied[1:]

    gathered, gain_all = (
        lax.all_gather(tokens, "tensor", axis=1, tiled=True),
        lax.all_gather(norm_gain, "tensor", axis=0, tiled=True),
    )
    floats = gathered.astype(jnp.float32)
    mean_square = jnp.mean(floats * floats, axis=-1, keepdims=True)
    normed = (floats * lax.rsqrt(mean_square + 1e-05) * gain_all.astype(jnp.float32)).astype(
        jnp.bfloat16
    )

    def features_of(index):
        fixed = index & mine(far_bits)
        parts = []
        for place_at in range(group):
            owner = fixed + place_at // 2 * 8 + place_at % 2 * mine(weight_bit)
            parts.append(lax.dynamic_slice_in_dim(normed, owner * shard_rows, shard_rows, 1))
        return jnp.concatenate(parts, axis=1)

    sends = [features_of(me ^ mine(masks)) for masks in (far_bits, z_bit, sum_bit)]
    x_own = features_of(me)
    x_far, x_z, x_a = [swap(v, m) for v, m in zip(sends, (far_bits, z_bit, sum_bit))]

    slot_table = dict(zip(offsets, slots_from))

    def put(masks, row, blocks, dense):
        where = jnp.concatenate(
            [
                (position(me ^ mine(masks)) * rows_here + row).reshape(1).astype(jnp.int32),
                slot_table[masks][row : row + blocks.shape[0] // BS].reshape(-1),
            ]
        )
        return place(where, blocks, dense, group * shard_rows, column_blocks)

    def plus(masks, more):
        return (masks[0] ^ more[0], masks[1] ^ more[1])

    near = swap(kept_blocks, weight_bit)
    chunks = []
    held = {(0, 0): kept_blocks}
    for masks in across:
        for known in list(held):
            held[plus(known, masks)] = swap(held[known], masks)
    del held[(0, 0)]
    chunks.append(held)
    dense = put((0, 0), 0, kept_blocks, None)
    late = []
    for row, held in enumerate(chunks):
        names = list(held)
        tied = lax.optimization_barrier([held[name] for name in names] + [dense])
        dense = tied[-1]
        if row == 0:
            dense = put(weight_bit, 0, near, dense)
        for masks, blocks, row_of in late:
            dense = put(masks, row_of, blocks, dense)
        late = []
        for name, blocks in zip(names, tied):
            late.append((plus(name, weight_bit), swap(blocks, weight_bit), row))
            dense = put(name, row, blocks, dense)
    for masks, blocks, row_of in late:
        dense = put(masks, row_of, blocks, dense)

    def product(left):
        return jnp.dot(left, dense, preferred_element_type=jnp.float32)

    half = column_blocks * BS // 2
    far = product(x_far).astype(jnp.bfloat16)
    far_first = swap(far[:, :half], sum_bit)
    far_second = swap(far[:, half:], sum_bit)
    far, x_z, x_a, x_own = lax.optimization_barrier((far, x_z, x_a, x_own))
    both = product(jnp.concatenate([x_z, x_a], axis=0))
    part_z = both[: x_z.shape[0]]
    part_a = both[x_z.shape[0] :].astype(jnp.bfloat16)
    a_first = swap(part_a[:, :half], sum_bit)
    a_second = swap(part_a[:, half:], sum_bit)
    sum_first = (part_z[:, :half] + far_first.astype(jnp.float32)).astype(jnp.bfloat16)
    sum_first, far_second = lax.optimization_barrier((sum_first, far_second))
    z_first = swap(sum_first, z_bit)
    sum_second = (part_z[:, half:] + far_second.astype(jnp.float32)).astype(jnp.bfloat16)
    z_second = swap(sum_second, z_bit)
    return finish(product(x_own), a_first, a_second, z_first, z_second)


def solution(mesh):
    in_specs = (
        P("dp", "tensor"),
        P("tensor"),
        P("dp", "tensor"),
        P("dp", "tensor"),
        P("dp", "tensor"),
    )
    out_specs = P("dp", "tensor")
    return jax.shard_map(
        per_device, mesh=mesh, in_specs=in_specs, out_specs=out_specs, check_vma=False
    )
```

```python
import functools

import jax
import jax.numpy as jnp
from jax import lax
from jax.experimental import pallas as pl
from jax.experimental.pallas import tpu as pltpu
from jax.sharding import PartitionSpec as P

KVH = 8
GROUP = 8
HD = 128
BS = 128


rope_theta = 500000.0


def place_body(where_ref, blocks_ref, *rest, slots, column_blocks):
    out_ref = rest[-1]
    row = pl.program_id(0)
    for column in range(column_blocks):
        slot = where_ref[1 + row * column_blocks + column]
        start = pl.multiple_of(jnp.minimum(slot, slots - 1) * BS, BS)
        block = blocks_ref[:, pl.ds(start, BS)]
        out_ref[:, column * BS : (column + 1) * BS] = jnp.where(
            slot < slots, block, jnp.zeros_like(block)
        )


def place(where, blocks, dense, total_rows, column_blocks):
    rows, width = blocks.shape
    slots = width // BS
    in_specs = [pl.BlockSpec((BS, width), lambda r, where: (r, 0))]
    operands = [where, blocks]
    aliases = {}
    if dense is not None:
        in_specs.append(pl.BlockSpec(memory_space=pl.ANY))
        operands.append(dense)
        aliases = {2: 0}
    return pl.pallas_call(
        functools.partial(place_body, slots=slots, column_blocks=column_blocks),
        grid_spec=pltpu.PrefetchScalarGridSpec(
            num_scalar_prefetch=1,
            grid=(rows // BS,),
            in_specs=in_specs,
            out_specs=pl.BlockSpec((BS, column_blocks * BS), lambda r, where: (where[0] + r, 0)),
        ),
        out_shape=jax.ShapeDtypeStruct((total_rows, column_blocks * BS), jnp.bfloat16),
        input_output_aliases=aliases,
        compiler_params=pltpu.CompilerParams(vmem_limit_bytes=56 * 1024 * 1024),
        cost_estimate=pl.CostEstimate(
            flops=0, bytes_accessed=rows * (width + column_blocks * BS) * 2, transcendentals=0
        ),
    )(*operands)


def finish_body(own, a_first, a_second, z_first, z_second, cosine, sine, out_ref, *, steps, heads):
    step = pl.program_id(0)
    cos_here = cosine[...]
    sin_here = sine[...]

    def write(from_a, from_z):
        for head in range(heads):
            lanes = slice(head * HD, (head + 1) * HD)
            mixed = (
                own[:, lanes]
                + from_a[:, lanes].astype(jnp.float32)
                + from_z[:, lanes].astype(jnp.float32)
            )
            turned = mixed * cos_here + pltpu.roll(mixed, HD // 2, 1) * sin_here
            rotated = (step * heads + head) % (GROUP + 2) < GROUP + 1
            out_ref[:, lanes] = jnp.where(rotated, turned, mixed).astype(jnp.bfloat16)

    @pl.when(step < steps // 2)
    def _():
        write(a_first, z_first)

    @pl.when(step >= steps // 2)
    def _():
        write(a_second, z_second)


def finish(own, a_first, a_second, z_first, z_second):
    rows, width = own.shape
    heads = (GROUP + 2) // 2
    block = heads * HD
    steps = width // block
    half_steps = steps // 2
    half_size = HD // 2
    inverse_freq = rope_theta ** (-(jnp.arange(half_size).astype(jnp.float32) * 2.0 / HD))
    angles = jnp.arange(rows).astype(jnp.float32)[:, None] * inverse_freq[None, :]
    cosine = jnp.cos(angles)
    sine = jnp.sin(angles)
    cos_full = jnp.concatenate([cosine, cosine], axis=-1)
    sin_full = jnp.concatenate([-sine, sine], axis=-1)
    low = pl.BlockSpec((rows, block), lambda j: (0, jnp.minimum(j, half_steps - 1)))
    high = pl.BlockSpec((rows, block), lambda j: (0, jnp.maximum(j - half_steps, 0)))
    table = pl.BlockSpec((rows, HD), lambda j: (0, 0))
    return pl.pallas_call(
        functools.partial(finish_body, steps=steps, heads=heads),
        grid=(steps,),
        in_specs=[pl.BlockSpec((rows, block), lambda j: (0, j)), low, high, low, high, table, table],
        out_specs=pl.BlockSpec((rows, block), lambda j: (0, j)),
        out_shape=jax.ShapeDtypeStruct((rows, width), jnp.bfloat16),
        compiler_params=pltpu.CompilerParams(vmem_limit_bytes=48 * 1024 * 1024),
        cost_estimate=pl.CostEstimate(
            flops=rows * width * 6, bytes_accessed=rows * width * 10, transcendentals=0
        ),
    )(own, a_first, a_second, z_first, z_second, cos_full, sin_full)


def per_device(tokens, norm_gain, kept_blocks, block_cols, row_counts):
    tensor_count = lax.axis_size("tensor")
    devices = lax.axis_size("dp")
    me = lax.axis_index("dp")
    column_blocks = KVH // tensor_count * (GROUP + 2) * HD // BS
    rows_here, slots = block_cols.shape
    shard_rows = rows_here * BS
    group = devices // 4
    odd = lax.axis_index("tensor") % 2
    z_bit = (4, 4)
    sum_bit = (2, 1)
    weight_bit = (1, 2)
    far_bits = (6, 5)
    across = [(1 << b, 1 << b) for b in range(devices.bit_length() - 2, 2, -1)]

    def swap(value, masks):
        pairs = [
            (i * tensor_count + t, (i ^ masks[t % 2]) * tensor_count + t)
            for i in range(devices)
            for t in range(tensor_count)
        ]
        return lax.ppermute(value, ("dp", "tensor"), pairs)

    def mine(masks):
        return jnp.where(odd == 1, masks[1], masks[0])

    def position(index):
        return index // 8 * 2 + jnp.where(index & mine(weight_bit) > 0, 1, 0)

    offsets = [(0, 0)]
    for masks in across:
        offsets += [(e ^ masks[0], o ^ masks[1]) for e, o in offsets]
    offsets += [(e ^ weight_bit[0], o ^ weight_bit[1]) for e, o in offsets]

    slot_of = jnp.where(
        (block_cols[:, None, :] == jnp.arange(column_blocks)[None, :, None])
        & (jnp.arange(slots)[None, None, :] < row_counts[:, :, None]),
        jnp.arange(slots)[None, None, :] - slots,
        0,
    )
    slot_of = (jnp.sum(slot_of, axis=-1) + slots).astype(jnp.int32)
    slots_from = [slot_of] + [swap(slot_of, masks) for masks in offsets[1:]]
    tied = lax.optimization_barrier([kept_blocks] + slots_from)
    kept_blocks, slots_from = tied[0], tied[1:]

    gathered, gain_all = (
        lax.all_gather(tokens, "tensor", axis=1, tiled=True),
        lax.all_gather(norm_gain, "tensor", axis=0, tiled=True),
    )
    floats = gathered.astype(jnp.float32)
    mean_square = jnp.mean(floats * floats, axis=-1, keepdims=True)
    normed = (floats * lax.rsqrt(mean_square + 1e-05) * gain_all.astype(jnp.float32)).astype(
        jnp.bfloat16
    )

    def features_of(index):
        fixed = index & mine(far_bits)
        parts = []
        for place_at in range(group):
            owner = fixed + place_at // 2 * 8 + place_at % 2 * mine(weight_bit)
            parts.append(lax.dynamic_slice_in_dim(normed, owner * shard_rows, shard_rows, 1))
        return jnp.concatenate(parts, axis=1)

    sends = [features_of(me ^ mine(masks)) for masks in (far_bits, z_bit, sum_bit)]
    x_own = features_of(me)
    x_far, x_z, x_a = [swap(v, m) for v, m in zip(sends, (far_bits, z_bit, sum_bit))]

    slot_table = dict(zip(offsets, slots_from))

    def put(masks, row, blocks, dense):
        where = jnp.concatenate(
            [
                (position(me ^ mine(masks)) * rows_here + row).reshape(1).astype(jnp.int32),
                slot_table[masks][row : row + blocks.shape[0] // BS].reshape(-1),
            ]
        )
        return place(where, blocks, dense, group * shard_rows, column_blocks)

    def plus(masks, more):
        return (masks[0] ^ more[0], masks[1] ^ more[1])

    near = swap(kept_blocks, weight_bit)
    chunks = []
    for row in range(rows_here):
        held = {(0, 0): kept_blocks[row * BS : (row + 1) * BS]}
        for masks in across:
            for known in list(held):
                held[plus(known, masks)] = swap(held[known], masks)
        del held[(0, 0)]
        chunks.append(held)
    dense = put((0, 0), 0, kept_blocks, None)
    late = []
    tie = list(sends)
    for row, held in enumerate(chunks):
        names = list(held)
        tied = lax.optimization_barrier([held[name] for name in names] + tie + [dense])
        dense = tied[-1]
        tie = []
        if row == 1 or rows_here == 1:
            dense = put(weight_bit, 0, near, dense)
        for masks, blocks, row_of in late:
            dense = put(masks, row_of, blocks, dense)
        late = []
        for name, blocks in zip(names, tied):
            late.append((plus(name, weight_bit), swap(blocks, weight_bit), row))
            dense = put(name, row, blocks, dense)
    for masks, blocks, row_of in late:
        dense = put(masks, row_of, blocks, dense)

    def product(left):
        return jnp.dot(left, dense, preferred_element_type=jnp.float32)

    half = column_blocks * BS // 2
    far = product(x_far).astype(jnp.bfloat16)
    far_first = swap(far[:, :half], sum_bit)
    far_second = swap(far[:, half:], sum_bit)
    far, x_z, x_a, x_own = lax.optimization_barrier((far, x_z, x_a, x_own))
    both = product(jnp.concatenate([x_z, x_a], axis=0))
    part_z = both[: x_z.shape[0]]
    part_a = both[x_z.shape[0] :].astype(jnp.bfloat16)
    a_first = swap(part_a[:, :half], sum_bit)
    a_second = swap(part_a[:, half:], sum_bit)
    sum_first = (part_z[:, :half] + far_first.astype(jnp.float32)).astype(jnp.bfloat16)
    sum_first, far_second = lax.optimization_barrier((sum_first, far_second))
    z_first = swap(sum_first, z_bit)
    sum_second = (part_z[:, half:] + far_second.astype(jnp.float32)).astype(jnp.bfloat16)
    z_second = swap(sum_second, z_bit)
    return finish(product(x_own), a_first, a_second, z_first, z_second)


def solution(mesh):
    in_specs = (
        P("dp", "tensor"),
        P("tensor"),
        P("dp", "tensor"),
        P("dp", "tensor"),
        P("dp", "tensor"),
    )
    out_specs = P("dp", "tensor")
    return jax.shard_map(
        per_device, mesh=mesh, in_specs=in_specs, out_specs=out_specs, check_vma=False
    )
```
